128 devices in a mesh: crop: 2 (over x_lo), row: 64 (over z, y, x_hi, core).
Axes of the slice: x: 4 (x_hi: 2, x_lo: 2; x = x_hi * 2 + x_lo), y: 4, z: 4, core: 2. Of those that a mesh axis runs over, the one named last changes fastest.
Arguments:
- pair: bfloat16 [1024, 512, 128], P(('crop', 'row')), parts along dimension 0, may hold values from -6 to 6
- labels: int32 [1024, 512], P(('crop', 'row')), parts along dimension 0, may hold values from 0 to 63, as said below
- crop_length: int32 [2], P('crop'), parts along dimension 0, may hold values from 256 to 512
- in_gain: float32 [128], replicated, may hold values from 0.5 to 1.5
- in_bias: float32 [128], replicated, may hold values from -1.75 to 1.75
- proj_weight: bfloat16 [128, 512], replicated, may hold values from -0.5 to 0.5
- proj_bias: float32 [512], replicated, may hold values from -3 to 3
- gate_weight: bfloat16 [128, 128], replicated, may hold values from -0.5 to 0.5
- gate_bias: float32 [128], replicated, may hold values from -3 to 3
- mid_gain: float32 [128], replicated, may hold values from 0.5 to 1.5
- mid_bias: float32 [128], replicated, may hold values from -1.75 to 1.75
- out_weight: bfloat16 [128, 128], replicated, may hold values from -0.5 to 0.5
- out_shift: float32 [128], replicated, may hold values from -1.75 to 1.75
- dist_weight: bfloat16 [128, 64], replicated, may hold values from -33 to 33
- dist_bias: float32 [64], replicated, may hold values from -6 to 6
Outputs:
- pair_grad: bfloat16 [1024, 512, 128], P(('crop', 'row')), parts along dimension 0
- loss: float32 [2], P('crop'), parts along dimension 0
The draws below stay inside these ranges and needn't reach their ends.
There are 2 independent parts, one for each index of `crop`. The reference program is written for one: setup_inputs(seed, part) draws one part's arguments, and reference() takes and returns one part's arrays. A program takes and returns all parts, laid end to end along the dimension named above; an argument that names none is the same for every part. Nothing has to cross between parts.
Inputs may be any that keep to these rules, and one draw needn't show every extreme that they name: labels[i, j] equals labels[j, i].
All inputs are finite; a program needn't handle non-finite values.
Results may differ from the reference program's by a relative error of at most 0.025.
Values may be sent and summed in bfloat16 or wider, within the bound.
A program may use at most 64 MiB of HBM per device.

```python
import jax
import jax.numpy as jnp
from jax import lax

N = 512
C = 128
H = 128
BINS = 64


def draw_labels(key, part):
    key = jax.random.fold_in(key, 3)
    raw = jax.random.randint(key, (N, N), 0, BINS, dtype=jnp.int32)
    rows = lax.broadcasted_iota(jnp.int32, (N, N), 0)
    cols = lax.broadcasted_iota(jnp.int32, (N, N), 1)
    return jnp.where(rows <= cols, raw, raw.T)


def draw_dist_weight(key, part):
    key = jax.random.fold_in(key, 5)
    key_base = jax.random.fold_in(key, 0)
    base = jax.random.normal(key_base, (C, BINS), jnp.float32) * C ** (-0.5)
    return base.astype(jnp.bfloat16)


def steps_of(stream_key, dims, cuts, low, largest):
    loudness = 1.0
    for axis_at, blocks in cuts:
        heights = jax.random.uniform(jax.random.fold_in(jax.random.fold_in(stream_key, 6), axis_at), (blocks,), jnp.float32, low / len(cuts), largest / len(cuts))
        loudness = loudness * jnp.repeat(jnp.exp(heights), dims[axis_at] // blocks).reshape((-1,) + (1,) * (len(dims) - 1 - axis_at))
    return loudness


def gaussian(rng, shape, width, most, cuts=(), kind=jnp.bfloat16):
    loudness = steps_of(rng, shape, cuts, -0.22, 0.18) if cuts else 1.0
    result = jax.random.normal(rng, shape, jnp.float32) * width * loudness
    return jnp.minimum(jnp.maximum(result, -most), most).astype(kind)


def setup_inputs(seed: int = 0, part: int = 0) -> dict:
    key_of = jax.random.split(jax.random.key(seed), 16)
    own_keys = jax.random.split(jax.random.fold_in(key_of[15], part), 16)
    pair = gaussian(own_keys[0], (N, N, C), 1.0, 6.0, ((0, 64),))
    labels = draw_labels(jax.random.fold_in(jax.random.fold_in(key_of[15], part), 71), part)
    crop_length = jax.random.randint(own_keys[2], (1,), N // 2, N + 1).astype(jnp.int32)
    in_gain = jnp.clip(1.0 + 0.1 * jax.random.normal(key_of[3], (C,), jnp.float32), 0.5, 1.5)
    in_bias = gaussian(key_of[4], (C,), 0.3, 1.75, (), jnp.float32)
    proj_weight = gaussian(key_of[5], (C, 4 * H), C ** -0.5, 0.5)
    proj_bias = gaussian(key_of[6], (4 * H,), 0.5, 3.0, (), jnp.float32)
    gate_weight = gaussian(key_of[7], (C, C), C ** -0.5, 0.5)
    gate_bias = gaussian(key_of[8], (C,), 0.5, 3.0, (), jnp.float32)
    mid_gain = jnp.clip(1.0 + 0.1 * jax.random.normal(key_of[9], (H,), jnp.float32), 0.5, 1.5)
    mid_bias = gaussian(key_of[10], (H,), 0.3, 1.75, (), jnp.float32)
    out_weight = gaussian(key_of[11], (H, C), H ** -0.5, 0.5)
    out_shift = gaussian(key_of[12], (C,), 0.3, 1.75, (), jnp.float32)
    dist_weight = draw_dist_weight(jax.random.fold_in(key_of[15], 71), part)
    dist_bias = gaussian(key_of[14], (BINS,), 1.0, 6.0, (), jnp.float32)
    return dict(pair=pair, labels=labels, crop_length=crop_length, in_gain=in_gain, in_bias=in_bias, proj_weight=proj_weight, proj_bias=proj_bias, gate_weight=gate_weight, gate_bias=gate_bias, mid_gain=mid_gain, mid_bias=mid_bias, out_weight=out_weight, out_shift=out_shift, dist_weight=dist_weight, dist_bias=dist_bias)


def layer_norm(values, gain, shift, axis):
    mean = lax.optimization_barrier(jnp.mean(values, axis=axis, keepdims=True))
    spread = lax.optimization_barrier(jnp.mean((values - mean) ** 2, axis=axis, keepdims=True))
    return (values - mean) * lax.rsqrt(spread + 1e-05) * gain + shift

def project_planes(values, row_start, length, in_gain, in_bias, proj_weight, proj_bias):
    hidden = proj_weight.shape[1] // 4
    normed = layer_norm(values, in_gain, in_bias, -1).astype(jnp.bfloat16)
    proj = jnp.einsum('rnc,ch->hrn', normed.astype(jnp.float32), proj_weight.astype(jnp.float32)) + proj_bias[:, None, None]
    shape = (values.shape[0], values.shape[1])
    row_ids = row_start + lax.broadcasted_iota(jnp.int32, shape, 0)
    col_ids = lax.broadcasted_iota(jnp.int32, shape, 1)
    keep = ((row_ids < length) & (col_ids < length)).astype(jnp.float32)
    left = jax.nn.sigmoid(proj[:hidden]) * proj[hidden:2 * hidden] * keep
    right = jax.nn.sigmoid(proj[2 * hidden:3 * hidden]) * proj[3 * hidden:] * keep
    return (left.astype(jnp.bfloat16), right.astype(jnp.bfloat16))

def mix_back(planes, values, in_gain, in_bias, gate_weight, gate_bias, mid_gain, mid_bias, out_weight, out_shift):
    normed = layer_norm(planes.astype(jnp.float32), mid_gain[:, None, None], mid_bias[:, None, None], 0).astype(jnp.bfloat16)
    update = jnp.einsum('hrn,hc->rnc', normed.astype(jnp.float32), out_weight.astype(jnp.float32)) + out_shift
    pair_norm = layer_norm(values, in_gain, in_bias, -1).astype(jnp.bfloat16)
    gate = jax.nn.sigmoid(jnp.einsum('rnc,cd->rnd', pair_norm.astype(jnp.float32), gate_weight.astype(jnp.float32)) + gate_bias)
    return (values + gate * update).astype(jnp.bfloat16)

def reference(pair, labels, crop_length, in_gain, in_bias, proj_weight, proj_bias, gate_weight, gate_bias, mid_gain, mid_bias, out_weight, out_shift, dist_weight, dist_bias):
    length = crop_length[0]
    block = 64
    blocks = N // block
    starts = jnp.arange(blocks, dtype=jnp.int32) * block
    full = pair.astype(jnp.float32)

    def first(values, start):
        return project_planes(values, start, length, in_gain, in_bias, proj_weight, proj_bias)

    def second(planes, values):
        return mix_back(planes, values, in_gain, in_bias, gate_weight, gate_bias, mid_gain, mid_bias, out_weight, out_shift)

    def forward_planes(start):
        values = lax.dynamic_slice_in_dim(full, start, block, 0)
        return first(values, start)
    lefts, rights = lax.map(forward_planes, starts)
    left_all = jnp.transpose(lefts, (1, 0, 2, 3)).reshape(H, N, N)
    right_all = jnp.transpose(rights, (1, 0, 2, 3)).reshape(H, N, N)

    def channel_product(planes):
        return jnp.dot(planes[0], planes[1].T, preferred_element_type=jnp.float32).astype(jnp.bfloat16)
    product = lax.map(channel_product, (left_all, right_all))

    def forward_logits(start):
        values = lax.dynamic_slice_in_dim(full, start, block, 0)
        planes = lax.dynamic_slice_in_dim(product, start, block, 1)
        updated = second(planes, values)
        logit_block = jnp.einsum('rnc,cb->rbn', updated.astype(jnp.float32), dist_weight.astype(jnp.float32)) + dist_bias[None, :, None]
        return logit_block.astype(jnp.bfloat16)
    logits = lax.map(forward_logits, starts).reshape(N, BINS, N)
    flipped = jnp.transpose(logits, (2, 1, 0))
    sym = logits.astype(jnp.float32) + flipped.astype(jnp.float32)
    logp = jax.nn.log_softmax(sym, axis=1)
    onehot = (labels[:, None, :] == lax.broadcasted_iota(jnp.int32, (1, BINS, 1), 1)).astype(jnp.float32)
    row_ids = lax.broadcasted_iota(jnp.int32, (N, N), 0)
    col_ids = lax.broadcasted_iota(jnp.int32, (N, N), 1)
    live = (row_ids < length) & (col_ids < length) & (row_ids != col_ids)
    upper = live & (col_ids > row_ids)
    terms = -lax.optimization_barrier(jnp.sum(onehot * logp, axis=1))
    loss_sum = jnp.sum(jnp.where(upper, terms, 0.0))
    present = length.astype(jnp.float32)
    loss = (loss_sum / (present * (present - 1.0) / 2.0)).reshape(1)
    residue = jnp.where(live[:, None, :], jnp.exp(logp) - onehot, 0.0).astype(jnp.bfloat16)

    def backward_mix(start):
        values = lax.dynamic_slice_in_dim(full, start, block, 0)
        planes = lax.dynamic_slice_in_dim(product, start, block, 1)
        res_block = lax.dynamic_slice_in_dim(residue, start, block, 0)
        cot = jnp.einsum('rbn,cb->rnc', res_block.astype(jnp.float32), dist_weight.astype(jnp.float32)).astype(jnp.bfloat16)
        unused, pull = jax.vjp(second, planes, values)
        return pull(cot)
    grad_planes, grad_mix = lax.map(backward_mix, starts)
    grad_product = jnp.transpose(grad_planes, (1, 0, 2, 3)).reshape(H, N, N)
    grad_mix = grad_mix.reshape(N, N, C)

    def channel_back(items):
        grad_h, left_h, right_h = items
        grad_l = jnp.dot(grad_h, right_h, preferred_element_type=jnp.float32).astype(jnp.bfloat16)
        grad_r = jnp.dot(grad_h.T, left_h, preferred_element_type=jnp.float32).astype(jnp.bfloat16)
        return (grad_l, grad_r)
    grad_left, grad_right = lax.map(channel_back, (grad_product, left_all, right_all))

    def backward_first(start):
        values = lax.dynamic_slice_in_dim(full, start, block, 0)
        cot_left = lax.dynamic_slice_in_dim(grad_left, start, block, 1)
        cot_right = lax.dynamic_slice_in_dim(grad_right, start, block, 1)
        unused, pull = jax.vjp(lambda v: first(v, start), values)
        return pull((cot_left, cot_right))[0]
    grad_first = lax.map(backward_first, starts).reshape(N, N, C)
    return ((grad_first + grad_mix).astype(jnp.bfloat16), loss)
```

```python
import jax
import jax.numpy as jnp
from jax import lax
from jax.experimental import pallas as pl
from jax.experimental.pallas import tpu as pltpu
from jax.sharding import PartitionSpec as P

MESH = pl.DeviceIdType.MESH
F32 = jnp.float32
BF16 = jnp.bfloat16
DEV = 64
ROWS = 8
N = 512
HALF = 256
CH = 128
BINS = 64


def dot(a, b):
    return jnp.dot(a, b, preferred_element_type=F32)


def spaced_store(ref, at, x):
    for t in range(x.shape[1] // 128):
        ref.at[t][pl.ds(at, CH, 16), :] = x[:, t * 128 : (t + 1) * 128]


def spaced_load(ref, at, runs):
    return jnp.concatenate([ref.at[t][pl.ds(at, CH, 16), :] for t in range(runs)], axis=1)


def tile_load(ref, at, runs):
    rows = pl.ds(pl.multiple_of(at, 16), 16)
    return jnp.concatenate([ref[t, rows, :] for t in range(runs)], axis=1)


def tile_store(ref, at, x):
    rows = pl.ds(pl.multiple_of(at, 16), 16)
    for t in range(x.shape[1] // 128):
        ref[t, rows, :] = x[:, t * 128 : (t + 1) * 128]


def partner(me, step):
    depth = lax.rem(lax.div(me, 16) + step, 4)
    height = lax.rem(lax.div(me, 4) + lax.div(step, 4) + step, 4)
    rest = lax.rem(me + lax.div(step, 16) + lax.div(step, 4) + step, 4)
    return depth * 16 + height * 4 + rest


def kernel(
    length_ref,
    pair_ref,
    labels_ref,
    in_gain_ref,
    in_bias_ref,
    proj_weight_ref,
    proj_bias_ref,
    gate_weight_ref,
    gate_bias_ref,
    mid_gain_ref,
    mid_bias_ref,
    out_weight_ref,
    out_shift_ref,
    dist_weight_ref,
    dist_bias_ref,
    grad_ref,
    loss_ref,
    values,
    in_hat,
    in_scale,
    normed,
    opened,
    amount,
    wide,
    send_planes,
    recv_planes,
    left_ch,
    right_ch,
    send_product,
    recv_product,
    mid,
    mid_hat,
    mid_scale,
    update,
    gate,
    logits,
    send_logits,
    recv_logits,
    flat_logits,
    order,
    cot,
    send_grad,
    recv_grad,
    grad_ch,
    send_back,
    recv_back,
    stack,
    part,
    parts,
    proj_t,
    gate_t,
    out_t,
    dist_t,
    back_weight,
    columns,
    proj_column,
    dist_column,
    send_sem,
    recv_sem,
):
    me = lax.axis_index("row")
    length = length_ref[0]
    first_row = me * ROWS

    def greet(step, carry):
        pl.semaphore_signal(
            pltpu.get_barrier_semaphore(),
            inc=1,
            device_id={"row": partner(me, step)},
            device_id_type=MESH,
        )
        return carry

    lax.fori_loop(1, DEV, greet, 0)

    def send(slot, source, target):
        def one(step, carry):
            peer = partner(me, step)
            pltpu.make_async_remote_copy(
                src_ref=source(peer),
                dst_ref=target,
                send_sem=send_sem.at[slot],
                recv_sem=recv_sem.at[slot],
                device_id={"row": peer},
                device_id_type=MESH,
            ).start()
            return carry

        lax.fori_loop(1, DEV, one, 0)

    def drain(slot, blocks, received):
        pltpu.make_async_copy(
            blocks, blocks, recv_sem.at[slot] if received else send_sem.at[slot]
        ).wait()

    def column(ref, out, at, size):
        out[pl.ds(at, size), :] = jnp.broadcast_to(ref[...], (8, size)).T[:, 0:1]

    column(in_gain_ref, columns, 0, CH)
    column(in_bias_ref, columns, CH, CH)
    column(gate_bias_ref, columns, 2 * CH, CH)
    column(mid_gain_ref, columns, 3 * CH, CH)
    column(mid_bias_ref, columns, 4 * CH, CH)
    column(out_shift_ref, columns, 5 * CH, CH)
    column(proj_bias_ref, proj_column, 0, 4 * CH)
    column(dist_bias_ref, dist_column, 0, BINS)
    proj_t[...] = proj_weight_ref[...].astype(F32).T.astype(BF16)
    gate_t[...] = gate_weight_ref[...].astype(F32).T.astype(BF16)
    out_t[...] = out_weight_ref[...].astype(F32).T.astype(BF16)
    dist_t[...] = dist_weight_ref[...].astype(F32).T.astype(BF16)
    back_weight[:, 0 : 4 * CH] = proj_weight_ref[...]
    back_weight[:, 4 * CH : 5 * CH] = gate_weight_ref[...]

    lane = lax.broadcasted_iota(jnp.int32, (1, N), 1)

    def kept(i):
        return jnp.where((lane < length) & (jnp.full((1, N), first_row + i) < length), 1.0, 0.0)

    def vec(k):
        return columns[pl.ds(k * CH, CH), :]

    def project(i, carry):
        x = pair_ref[i].astype(F32).T
        values[i] = x
        mean = jnp.mean(x, axis=0, keepdims=True)
        x = x - mean
        scale = lax.rsqrt(jnp.mean(x * x, axis=0, keepdims=True) + 1e-05)
        x = x * scale
        in_hat[i] = x
        in_scale[i] = scale
        norm = (x * vec(0) + vec(1)).astype(BF16)
        normed[i] = norm
        keep = kept(i)
        for side in range(2):
            at = 2 * CH * side
            proj = dot(proj_t[pl.ds(at, 2 * CH), :], norm) + proj_column[pl.ds(at, 2 * CH), :]
            open_ = jax.nn.sigmoid(proj[0:CH])
            opened[side, i] = open_
            amount[side, i] = proj[CH:]
            spaced_store(wide, side * ROWS + i, open_ * proj[CH:] * keep)
        return carry

    lax.fori_loop(0, ROWS, project, 0)

    pl.semaphore_wait(pltpu.get_barrier_semaphore(), DEV - 1)

    for odd in range(2):

        def pack(d, carry):
            send_planes[odd, d] = tile_load(wide, d * 32 + odd * 16, 4).astype(BF16)
            return carry

        lax.fori_loop(0, DEV, pack, 0)
        send(odd, lambda d: send_planes.at[odd, d], recv_planes.at[odd, me])
        recv_planes[odd, me] = send_planes[odd, me]

    def open_gate(i, carry):
        gate[i] = jax.nn.sigmoid(dot(gate_t[...], normed[i]) + vec(2))
        return carry

    lax.fori_loop(0, ROWS, open_gate, 0)
    row_at = lax.broadcasted_iota(jnp.int32, (N, N), 0)
    lane_at = lax.broadcasted_iota(jnp.int32, (N, N), 1)
    place = jnp.where(row_at < HALF, 2 * row_at, 2 * row_at - (N - 1))
    order[...] = jnp.where(place == lane_at, 1.0, 0.0).astype(BF16)

    for odd in range(2):
        drain(odd, recv_planes.at[odd, pl.ds(0, DEV - 1)], True)

        def unpack(b, carry):
            block = recv_planes[odd, pl.ds(b * 8, 8)].astype(F32).reshape(8, 2, 8, N)
            at = pl.ds(pl.multiple_of(b * 64, 64), 64)
            left_ch[odd, at, :] = block[:, 0].reshape(64, N).astype(BF16)
            right_ch[odd, at, :] = block[:, 1].reshape(64, N).astype(BF16)
            return carry

        lax.fori_loop(0, 8, unpack, 0)
        for half in range(2):
            product = lax.dot_general(
                left_ch[odd],
                right_ch[odd, half * HALF : (half + 1) * HALF, :],
                (((1,), (1,)), ((), ())),
                preferred_element_type=F32,
            )
            stack[:, half * 8 : half * 8 + 8, 0:HALF] = product.reshape(DEV, 8, HALF)
        send_product[odd] = stack[:, :, 0:HALF].astype(BF16)
        send(2 + odd, lambda d: send_product.at[odd, d], recv_product.at[odd, me])
        recv_product[odd, me] = send_product[odd, me]

    for odd in range(2):
        drain(2 + odd, recv_product.at[odd, pl.ds(0, DEV - 1)], True)

        def spread(s, carry):
            tile_store(mid, s * 32 + odd * 16, recv_product[odd, s].astype(F32))
            return carry

        lax.fori_loop(0, DEV, spread, 0)

    def mix(i, carry):
        x = jnp.concatenate([spaced_load(mid, i, 2), spaced_load(mid, 8 + i, 2)], axis=1)
        x = x - jnp.mean(x, axis=0, keepdims=True)
        scale = lax.rsqrt(jnp.mean(x * x, axis=0, keepdims=True) + 1e-05)
        x = x * scale
        mid_hat[i] = x
        mid_scale[i] = scale
        change = dot(out_t[...], (x * vec(3) + vec(4)).astype(BF16)) + vec(5)
        update[i] = change
        updated = (values[i] + gate[i] * change).astype(BF16)
        logits[i] = (dot(dist_t[...], updated) + dist_column[...]).astype(BF16).astype(F32)
        return carry

    lax.fori_loop(0, ROWS, mix, 0)

    for two in range(2):
        for low in range(2):
            p = 2 * two + low
            pairs = jnp.concatenate([logits[2 * p], logits[2 * p + 1]], axis=0).T
            stack[:, low * 8 : low * 8 + 8, 0:CH] = pairs.reshape(DEV, 8, CH)
        send_logits[:, two] = stack[:, :, 0:CH].astype(BF16)
    send(4, lambda d: send_logits.at[d], recv_logits.at[me])
    recv_logits[me] = send_logits[me]
    drain(4, recv_logits.at[pl.ds(0, DEV - 1)], True)
    flat_logits[...] = recv_logits[...].astype(F32).reshape(DEV * 32, CH)

    part[...] = jnp.zeros_like(part)
    bin_at = lax.broadcasted_iota(jnp.int32, (BINS, N), 0)

    def backward(i, carry):
        turned = flat_logits[pl.ds(i, HALF, 8), :].T.astype(BF16)
        turned = jnp.concatenate([turned[0:BINS], turned[BINS:]], axis=1)
        sym = logits[i] + dot(turned, order[...])
        sym = sym - jnp.max(sym, axis=0, keepdims=True)
        powers = jnp.exp(sym)
        logp = sym - jnp.log(jnp.sum(powers, axis=0, keepdims=True))
        hot = jnp.where(labels_ref[pl.ds(i, 1), :] == bin_at, 1.0, 0.0)
        row = jnp.full((1, N), first_row + i)
        live = (lane < length) & (row < length) & (lane != row)
        terms = -jnp.sum(hot * logp, axis=0, keepdims=True)
        terms = jnp.where(live & (lane > row), terms, 0.0)
        part[...] += (
            terms[:, 0:128] + terms[:, 128:256] + terms[:, 256:384] + terms[:, 384:512]
        )
        residue = jnp.where(live, jnp.exp(logp) - hot, 0.0).astype(BF16)
        back = dot(dist_weight_ref[...], residue).astype(BF16)
        cot[i] = back
        back = dot(out_weight_ref[...], (back.astype(F32) * gate[i]).astype(BF16)) * vec(3)
        hat = mid_hat[i]
        back = mid_scale[i] * (
            back
            - jnp.mean(back, axis=0, keepdims=True)
            - hat * jnp.mean(back * hat, axis=0, keepdims=True)
        )
        spaced_store(mid, i, back[:, 0:HALF])
        spaced_store(mid, 8 + i, back[:, HALF:])
        return carry

    lax.fori_loop(0, ROWS, backward, 0)

    for odd in range(2):

        def pack_grad(d, carry):
            send_grad[odd, d] = tile_load(mid, d * 32 + odd * 16, 2).astype(BF16)
            return carry

        lax.fori_loop(0, DEV, pack_grad, 0)
        send(5 + odd, lambda d: send_grad.at[odd, d], recv_grad.at[odd, me])
        recv_grad[odd, me] = send_grad[odd, me]

    parts[me] = part[...]
    send(7, lambda d: part, parts.at[me])

    for odd in range(2):
        drain(5 + odd, recv_grad.at[odd, pl.ds(0, DEV - 1)], True)

        def unpack_grad(b, carry):
            block = recv_grad[odd, pl.ds(b * 8, 8)].astype(F32).reshape(8, 2, 8, HALF)
            at = pl.ds(pl.multiple_of(b * 64, 64), 64)
            grad_ch[at, 0:HALF] = block[:, 0].reshape(64, HALF).astype(BF16)
            grad_ch[at, HALF:N] = block[:, 1].reshape(64, HALF).astype(BF16)
            return carry

        lax.fori_loop(0, 8, unpack_grad, 0)
        stack[:, 0:8, :] = dot(grad_ch[...], right_ch[odd]).reshape(DEV, 8, N)
        stack[:, 8:16, :] = lax.dot_general(
            grad_ch[...], left_ch[odd], (((0,), (0,)), ((), ())), preferred_element_type=F32
        ).reshape(DEV, 8, N)
        send_back[odd] = stack[...].astype(BF16)
        send(8 + odd, lambda d: send_back.at[odd, d], recv_back.at[odd, me])
        recv_back[odd, me] = send_back[odd, me]

    for odd in range(2):
        drain(8 + odd, recv_back.at[odd, pl.ds(0, DEV - 1)], True)

        def spread_back(s, carry):
            tile_store(wide, s * 32 + odd * 16, recv_back[odd, s].astype(F32))
            return carry

        lax.fori_loop(0, DEV, spread_back, 0)

    def finish(i, carry):
        keep = kept(i)
        pieces = []
        for side in range(2):
            grad = spaced_load(wide, side * ROWS + i, 4) * keep
            open_ = opened[side, i]
            grad = grad * open_
            pieces.append((grad * amount[side, i] * (1.0 - open_)).astype(BF16))
            pieces.append(grad.astype(BF16))
        back = cot[i].astype(F32)
        open_ = gate[i]
        pieces.append((back * update[i] * open_ * (1.0 - open_)).astype(BF16))
        grad = dot(back_weight[...], jnp.concatenate(pieces, axis=0)) * vec(0)
        hat = in_hat[i]
        grad = in_scale[i] * (
            grad
            - jnp.mean(grad, axis=0, keepdims=True)
            - hat * jnp.mean(grad * hat, axis=0, keepdims=True)
        )
        grad_ref[i] = (grad + back).T.astype(BF16)
        return carry

    lax.fori_loop(0, ROWS, finish, 0)

    drain(7, parts.at[pl.ds(0, DEV - 1)], True)
    total = jnp.sum(jnp.sum(parts[...], axis=0), axis=1, keepdims=True)
    present = jnp.full((1, 1), length).astype(F32)
    loss_ref[...] = jnp.broadcast_to(total / (present * (present - 1.0) / 2.0), (1, 128))

    for odd in range(2):
        drain(odd, send_planes.at[odd, pl.ds(0, DEV - 1)], False)
        drain(2 + odd, send_product.at[odd, pl.ds(0, DEV - 1)], False)
        drain(5 + odd, send_grad.at[odd, pl.ds(0, DEV - 1)], False)
        drain(8 + odd, send_back.at[odd, pl.ds(0, DEV - 1)], False)
    drain(4, send_logits.at[pl.ds(0, DEV - 1)], False)
    drain(7, parts.at[pl.ds(0, DEV - 1)], False)


SCRATCH = (
    ((ROWS, CH, N), F32),
    ((ROWS, CH, N), F32),
    ((ROWS, 1, N), F32),
    ((ROWS, CH, N), BF16),
    ((2, ROWS, CH, N), F32),
    ((2, ROWS, CH, N), F32),
    ((4, CH * 16, 128), F32),
    ((2, DEV, 16, N), BF16),
    ((2, DEV, 16, N), BF16),
    ((2, N, N), BF16),
    ((2, N, N), BF16),
    ((2, DEV, 16, HALF), BF16),
    ((2, DEV, 16, HALF), BF16),
    ((2, CH * 16, 128), F32),
    ((ROWS, CH, N), F32),
    ((ROWS, 1, N), F32),
    ((ROWS, CH, N), F32),
    ((ROWS, CH, N), F32),
    ((ROWS, BINS, N), F32),
    ((DEV, 2, 16, CH), BF16),
    ((DEV, 2, 16, CH), BF16),
    ((DEV * 32, CH), F32),
    ((N, N), BF16),
    ((ROWS, CH, N), BF16),
    ((2, DEV, 16, HALF), BF16),
    ((2, DEV, 16, HALF), BF16),
    ((N, N), BF16),
    ((2, DEV, 16, N), BF16),
    ((2, DEV, 16, N), BF16),
    ((DEV, 16, N), F32),
    ((1, 128), F32),
    ((DEV, 1, 128), F32),
    ((4 * CH, CH), BF16),
    ((CH, CH), BF16),
    ((CH, CH), BF16),
    ((BINS, CH), BF16),
    ((CH, 5 * CH), BF16),
    ((6 * CH, 1), F32),
    ((4 * CH, 1), F32),
    ((BINS, 1), F32),
)


def local(pair, labels, crop_length, *parameters):
    parameters = [p.reshape(1, -1) if p.ndim == 1 else p for p in parameters]
    grad, loss = pl.pallas_call(
        kernel,
        out_shape=(
            jax.ShapeDtypeStruct(pair.shape, BF16),
            jax.ShapeDtypeStruct((1, 128), F32),
        ),
        in_specs=[pl.BlockSpec(memory_space=pltpu.SMEM)]
        + [pl.BlockSpec(memory_space=pltpu.VMEM)] * (2 + len(parameters)),
        out_specs=[pl.BlockSpec(memory_space=pltpu.VMEM)] * 2,
        scratch_shapes=[pltpu.VMEM(shape, kind) for shape, kind in SCRATCH]
        + [pltpu.SemaphoreType.DMA((10,)), pltpu.SemaphoreType.DMA((10,))],
        compiler_params=pltpu.CompilerParams(
            collective_id=0, has_side_effects=True, vmem_limit_bytes=60 * 1024 * 1024
        ),
    )(crop_length, pair, labels, *parameters)
    return grad, loss[0, 0:1]


def solution(mesh):
    return jax.shard_map(
        local,
        mesh=mesh,
        in_specs=(P(("crop", "row"), None, None), P(("crop", "row"), None), P("crop")) + (P(),) * 12,
        out_specs=(P(("crop", "row"), None, None), P("crop")),
        check_vma=False,
    )
```

```python
import jax
import jax.numpy as jnp
from jax import lax
from jax.experimental import pallas as pl
from jax.experimental.pallas import tpu as pltpu
from jax.sharding import PartitionSpec as P

MESH = pl.DeviceIdType.MESH
F32 = jnp.float32
BF16 = jnp.bfloat16
DEV = 64
ROWS = 8
N = 512
HALF = 256
CH = 128
BINS = 64


def dot(a, b):
    return jnp.dot(a, b, preferred_element_type=F32)


def spaced_store(ref, at, x):
    for t in range(x.shape[1] // 128):
        ref.at[t][pl.ds(at, CH, 16), :] = x[:, t * 128 : (t + 1) * 128]


def tile_load(ref, runs, at, rows):
    rows = pl.ds(pl.multiple_of(at, 16), rows)
    return jnp.concatenate([ref[t, rows, :] for t in runs], axis=1)


def tile_store(ref, runs, at, x):
    rows = pl.ds(pl.multiple_of(at, 16), x.shape[0])
    for n, t in enumerate(runs):
        ref[t, rows, :] = x[:, n * 128 : (n + 1) * 128]


def each(count, body, unroll):
    def step(i, carry):
        body(i)
        return carry

    lax.fori_loop(0, count, step, 0, unroll=unroll)


def partner(me, step):
    depth = lax.rem(lax.div(me, 16) + step, 4)
    height = lax.rem(lax.div(me, 4) + lax.div(step, 4) + step, 4)
    rest = lax.rem(me + lax.div(step, 16) + lax.div(step, 4) + step, 4)
    return depth * 16 + height * 4 + rest


def kernel(
    length_ref,
    pair_ref,
    labels_ref,
    in_gain_ref,
    in_bias_ref,
    proj_weight_ref,
    proj_bias_ref,
    gate_weight_ref,
    gate_bias_ref,
    mid_gain_ref,
    mid_bias_ref,
    out_weight_ref,
    out_shift_ref,
    dist_turned_ref,
    dist_bias_ref,
    grad_ref,
    loss_ref,
    values,
    in_hat,
    in_scale,
    normed,
    opened,
    amount,
    wide,
    send_planes,
    recv_planes,
    send_rest,
    recv_rest,
    left_ch,
    right_ch,
    send_product,
    recv_product,
    send_second,
    recv_second,
    mid,
    mid_hat,
    mid_scale,
    update,
    gate,
    logits,
    stack,
    send_logits,
    recv_logits,
    flat_logits,
    order,
    cot,
    send_grad,
    recv_grad,
    grad_ch,
    send_back,
    recv_back,
    send_last,
    recv_last,
    part,
    parts,
    proj_t,
    gate_t,
    out_t,
    dist_weight,
    back_weight,
    columns,
    proj_column,
    dist_column,
    send_sem,
    recv_sem,
):
    me = lax.axis_index("row")
    length = length_ref[0]
    first_row = me * ROWS

    def greet(step, carry):
        pl.semaphore_signal(
            pltpu.get_barrier_semaphore(),
            inc=1,
            device_id={"row": partner(me, step)},
            device_id_type=MESH,
        )
        return carry

    lax.fori_loop(1, DEV, greet, 0)

    def send(slot, source, target, pack=None):
        def one(step, carry):
            peer = partner(me, step)
            if pack is not None:
                source.at[peer][...] = pack(peer)
            pltpu.make_async_remote_copy(
                src_ref=source.at[peer] if source.shape[0] == DEV else source,
                dst_ref=target.at[me],
                send_sem=send_sem.at[slot],
                recv_sem=recv_sem.at[slot],
                device_id={"row": peer},
                device_id_type=MESH,
            ).start()
            return carry

        lax.fori_loop(1, DEV, one, 0, unroll=3)
        if pack is not None:
            target.at[me][...] = pack(me)
        elif source.shape[0] == DEV:
            target.at[me][...] = source.at[me][...]
        else:
            target.at[me][...] = source[...]

    def arrived(slot, target):
        blocks = target.at[pl.ds(0, DEV - 1)]
        pltpu.make_async_copy(blocks, blocks, recv_sem.at[slot]).wait()

    def column(ref, out, at, size):
        out[pl.ds(at, size), :] = jnp.broadcast_to(ref[...], (8, size)).T[:, 0:1]

    column(in_gain_ref, columns, 0, CH)
    column(in_bias_ref, columns, CH, CH)
    column(proj_bias_ref, proj_column, 0, 4 * CH)
    proj_t[...] = proj_weight_ref[...].astype(F32).T.astype(BF16)

    lane = lax.broadcasted_iota(jnp.int32, (1, N), 1)

    def lanes(half):
        return slice(half * HALF, (half + 1) * HALF)

    def kept(i, half):
        row = jnp.full((1, HALF), first_row + i)
        return jnp.where((lane[:, lanes(half)] < length) & (row < length), 1.0, 0.0)

    def vec(k):
        return columns[pl.ds(k * CH, CH), :]

    def project(half):
        at = lanes(half)

        def body(i):
            x = pair_ref[i, at, :].astype(F32).T
            values[i, :, at] = x
            x = x - jnp.mean(x, axis=0, keepdims=True)
            scale = lax.rsqrt(jnp.mean(x * x, axis=0, keepdims=True) + 1e-05)
            x = x * scale
            in_hat[i, :, at] = x
            in_scale[i, :, at] = scale
            norm = (x * vec(0) + vec(1)).astype(BF16)
            normed[i, :, at] = norm
            keep = kept(i, half)
            for side in range(2):
                rows = pl.ds(2 * CH * side, 2 * CH)
                proj = dot(proj_t[rows, :], norm) + proj_column[rows, :]
                open_ = jax.nn.sigmoid(proj[0:CH])
                opened[side, i, :, at] = open_
                amount[side, i, :, at] = proj[CH:]
                spaced_store(
                    wide.at[pl.ds(2 * half, 2)], side * ROWS + i, open_ * proj[CH:] * keep
                )

        each(ROWS, body, ROWS)

    project(0)
    pl.semaphore_wait(pltpu.get_barrier_semaphore(), DEV - 1)
    send(
        0,
        send_planes,
        recv_planes,
        lambda d: tile_load(wide, (0, 1), d * 32, 32).astype(BF16).reshape(2, 16, HALF),
    )
    project(1)
    for odd in range(2):
        send(
            1 + odd,
            send_rest.at[odd],
            recv_rest.at[odd],
            lambda d: tile_load(wide, (2, 3), d * 32 + odd * 16, 16).astype(BF16),
        )

    column(gate_bias_ref, columns, 2 * CH, CH)
    column(mid_gain_ref, columns, 3 * CH, CH)
    column(mid_bias_ref, columns, 4 * CH, CH)
    column(out_shift_ref, columns, 5 * CH, CH)
    column(dist_bias_ref, dist_column, 0, BINS)
    gate_t[...] = gate_weight_ref[...].astype(F32).T.astype(BF16)
    out_t[...] = out_weight_ref[...].astype(F32).T.astype(BF16)
    dist_weight[...] = dist_turned_ref[...].astype(F32).T.astype(BF16)
    back_weight[:, 0 : 4 * CH] = proj_weight_ref[...]
    back_weight[:, 4 * CH : 5 * CH] = gate_weight_ref[...]
    row_at = lax.broadcasted_iota(jnp.int32, (N, N), 0)
    lane_at = lax.broadcasted_iota(jnp.int32, (N, N), 1)
    place = jnp.where(row_at < HALF, 2 * row_at, 2 * row_at - (N - 1))
    order[...] = jnp.where(place == lane_at, 1.0, 0.0).astype(BF16)

    def open_gate(i):
        gate[i] = jax.nn.sigmoid(dot(gate_t[...], normed[i]) + vec(2))

    each(ROWS, open_gate, 2)

    def unpack(odd, half, source):
        at = lanes(half)

        def body(b):
            block = source[pl.ds(b * 8, 8)].astype(F32).reshape(8, 2, 8, HALF)
            rows = pl.ds(pl.multiple_of(b * 64, 64), 64)
            left_ch[odd, rows, at] = block[:, 0].reshape(64, HALF).astype(BF16)
            right_ch[odd, rows, at] = block[:, 1].reshape(64, HALF).astype(BF16)

        each(8, body, 4)

    arrived(0, recv_planes)
    for odd in range(2):
        unpack(odd, 0, recv_planes.at[:, odd])

    def product(odd, half):
        x = lax.dot_general(
            left_ch[odd],
            right_ch[odd, lanes(half), :],
            (((1,), (1,)), ((), ())),
            preferred_element_type=F32,
        )
        return jnp.concatenate(
            [x[:, 0:128].reshape(DEV, 8, 128), x[:, 128:].reshape(DEV, 8, 128)], axis=1
        ).astype(BF16)

    arrived(1, recv_rest.at[0])
    unpack(0, 1, recv_rest.at[0])
    for half in range(2):
        send_product[:, half] = product(0, half)
    send(3, send_product, recv_product)
    arrived(2, recv_rest.at[1])
    unpack(1, 1, recv_rest.at[1])
    for half in range(2):
        send_second[half] = product(1, half)
        send(4 + half, send_second.at[half], recv_second.at[half])

    def mix(half):
        at = lanes(half)

        def body(i):
            x = jnp.concatenate(
                [mid.at[half][pl.ds(i, CH, 16), :], mid.at[half][pl.ds(8 + i, CH, 16), :]], axis=1
            )
            x = x - jnp.mean(x, axis=0, keepdims=True)
            scale = lax.rsqrt(jnp.mean(x * x, axis=0, keepdims=True) + 1e-05)
            x = x * scale
            mid_hat[i, :, at] = x
            mid_scale[i, :, at] = scale
            change = dot(out_t[...], (x * vec(3) + vec(4)).astype(BF16)) + vec(5)
            update[i, :, at] = change
            updated = (values[i, :, at] + gate[i, :, at] * change).astype(BF16)
            found = dot(dist_turned_ref[...], updated) + dist_column[...]
            logits[i, :, at] = found.astype(BF16).astype(F32)

        each(ROWS, body, 4)

    arrived(3, recv_product)
    for half in range(2):

        def spread(s):
            tile_store(mid, (half,), s * 32, recv_product[s, half].astype(F32))

        each(DEV, spread, 8)
    for half in range(2):
        arrived(4 + half, recv_second.at[half])

        def spread_second(s):
            tile_store(mid, (half,), s * 32 + 16, recv_second[half, s].astype(F32))

        each(DEV, spread_second, 8)
        mix(half)

    for two in range(2):
        for low in range(2):
            p = 2 * two + low
            pairs = jnp.concatenate([logits[2 * p], logits[2 * p + 1]], axis=0).T
            stack[:, low * 8 : low * 8 + 8, :] = pairs.reshape(DEV, 8, CH)
        send_logits[:, two] = stack[...].astype(BF16)
    send(6, send_logits, recv_logits)
    arrived(6, recv_logits)
    flat_logits[...] = recv_logits[...].astype(F32).reshape(DEV * 32, CH)

    part[...] = jnp.zeros_like(part)
    bin_at = lax.broadcasted_iota(jnp.int32, (BINS, HALF), 0)

    def backward(i):
        turned = flat_logits[pl.ds(i, HALF, 8), :].T.astype(BF16)
        turned = jnp.concatenate([turned[0:BINS], turned[BINS:]], axis=1)
        row = jnp.full((1, HALF), first_row + i)
        for half in range(2):
            at = lanes(half)
            sym = logits[i, :, at] + dot(turned, order[:, at])
            sym = sym - jnp.max(sym, axis=0, keepdims=True)
            logp = sym - jnp.log(jnp.sum(jnp.exp(sym), axis=0, keepdims=True))
            hot = jnp.where(labels_ref[pl.ds(i, 1), at] == bin_at, 1.0, 0.0)
            here = lane[:, at]
            live = (here < length) & (row < length) & (here != row)
            terms = -jnp.sum(hot * logp, axis=0, keepdims=True)
            terms = jnp.where(live & (here > row), terms, 0.0)
            part[...] += terms[:, 0:128] + terms[:, 128:]
            residue = jnp.where(live, jnp.exp(logp) - hot, 0.0).astype(BF16)
            back = dot(dist_weight[...], residue).astype(BF16)
            cot[i, :, at] = back
            back = (back.astype(F32) * gate[i, :, at]).astype(BF16)
            back = dot(out_weight_ref[...], back) * vec(3)
            hat = mid_hat[i, :, at]
            back = mid_scale[i, :, at] * (
                back
                - jnp.mean(back, axis=0, keepdims=True)
                - hat * jnp.mean(back * hat, axis=0, keepdims=True)
            )
            spaced_store(mid, half * 8 + i, back)

    each(ROWS, backward, ROWS)

    for odd in range(2):
        send(
            7 + odd,
            send_grad.at[odd],
            recv_grad.at[odd],
            lambda d: tile_load(mid, (0, 1), d * 32 + odd * 16, 16).astype(BF16),
        )
    send(9, part, parts)

    def planes_back(odd, half):
        at = lanes(half)
        x = dot(grad_ch[...], right_ch[odd, :, at]).reshape(DEV, 8, HALF)
        y = lax.dot_general(
            grad_ch[...], left_ch[odd, :, at], (((0,), (0,)), ((), ())), preferred_element_type=F32
        ).reshape(DEV, 8, HALF)
        return jnp.concatenate([x, y], axis=1).astype(BF16)

    for odd in range(2):
        arrived(7 + odd, recv_grad.at[odd])

        def unpack_grad(b):
            block = recv_grad[odd, pl.ds(b * 8, 8)].astype(F32).reshape(8, 2, 8, HALF)
            rows = pl.ds(pl.multiple_of(b * 64, 64), 64)
            grad_ch[rows, 0:HALF] = block[:, 0].reshape(64, HALF).astype(BF16)
            grad_ch[rows, HALF:N] = block[:, 1].reshape(64, HALF).astype(BF16)

        each(8, unpack_grad, 4)
        for half in range(2):
            if odd == 0:
                send_back[:, :, lanes(half)] = planes_back(odd, half)
            else:
                send_last[half] = planes_back(odd, half)
                send(11 + half, send_last.at[half], recv_last.at[half])
        if odd == 0:
            send(10, send_back, recv_back)

    def finish(half):
        at = lanes(half)

        def body(i):
            keep = kept(i, half)
            pieces = []
            for side in range(2):
                rows = pl.ds(side * ROWS + i, CH, 16)
                grad = jnp.concatenate(
                    [wide.at[2 * half][rows, :], wide.at[2 * half + 1][rows, :]], axis=1
                )
                open_ = opened[side, i, :, at]
                grad = grad * keep * open_
                pieces.append((grad * amount[side, i, :, at] * (1.0 - open_)).astype(BF16))
                pieces.append(grad.astype(BF16))
            back = cot[i, :, at].astype(F32)
            open_ = gate[i, :, at]
            pieces.append((back * update[i, :, at] * open_ * (1.0 - open_)).astype(BF16))
            grad = dot(back_weight[...], jnp.concatenate(pieces, axis=0)) * vec(0)
            hat = in_hat[i, :, at]
            grad = in_scale[i, :, at] * (
                grad
                - jnp.mean(grad, axis=0, keepdims=True)
                - hat * jnp.mean(grad * hat, axis=0, keepdims=True)
            )
            grad_ref[i, at, :] = (grad + back).T.astype(BF16)

        each(ROWS, body, ROWS)

    arrived(10, recv_back)

    def spread_back(s):
        tile_store(wide, (0, 1, 2, 3), s * 32, recv_back[s].astype(F32))

    each(DEV, spread_back, 8)
    for half in range(2):
        arrived(11 + half, recv_last.at[half])

        def spread_last(s):
            tile_store(
                wide, (2 * half, 2 * half + 1), s * 32 + 16, recv_last[half, s].astype(F32)
            )

        each(DEV, spread_last, 8)
        finish(half)

    arrived(9, parts)
    total = jnp.sum(jnp.sum(parts[...], axis=0), axis=1, keepdims=True)
    present = jnp.full((1, 1), length).astype(F32)
    loss_ref[...] = jnp.broadcast_to(total / (present * (present - 1.0) / 2.0), (1, 128))

    for slot, blocks in (
        (0, send_planes),
        (1, send_rest.at[0]),
        (2, send_rest.at[1]),
        (3, send_product),
        (4, send_second.at[0]),
        (5, send_second.at[1]),
        (6, send_logits),
        (7, send_grad.at[0]),
        (8, send_grad.at[1]),
        (9, parts),
        (10, send_back),
        (11, send_last.at[0]),
        (12, send_last.at[1]),
    ):
        blocks = blocks.at[pl.ds(0, DEV - 1)]
        pltpu.make_async_copy(blocks, blocks, send_sem.at[slot]).wait()


SCRATCH = (
    ((ROWS, CH, N), F32),
    ((ROWS, CH, N), F32),
    ((ROWS, 1, N), F32),
    ((ROWS, CH, N), BF16),
    ((2, ROWS, CH, N), F32),
    ((2, ROWS, CH, N), F32),
    ((4, CH * 16, 128), F32),
    ((DEV, 2, 16, HALF), BF16),
    ((DEV, 2, 16, HALF), BF16),
    ((2, DEV, 16, HALF), BF16),
    ((2, DEV, 16, HALF), BF16),
    ((2, N, N), BF16),
    ((2, N, N), BF16),
    ((DEV, 2, 16, 128), BF16),
    ((DEV, 2, 16, 128), BF16),
    ((2, DEV, 16, 128), BF16),
    ((2, DEV, 16, 128), BF16),
    ((2, CH * 16, 128), F32),
    ((ROWS, CH, N), F32),
    ((ROWS, 1, N), F32),
    ((ROWS, CH, N), F32),
    ((ROWS, CH, N), F32),
    ((ROWS, BINS, N), F32),
    ((DEV, 16, CH), F32),
    ((DEV, 2, 16, CH), BF16),
    ((DEV, 2, 16, CH), BF16),
    ((DEV * 32, CH), F32),
    ((N, N), BF16),
    ((ROWS, CH, N), BF16),
    ((2, DEV, 16, HALF), BF16),
    ((2, DEV, 16, HALF), BF16),
    ((N, N), BF16),
    ((DEV, 16, N), BF16),
    ((DEV, 16, N), BF16),
    ((2, DEV, 16, HALF), BF16),
    ((2, DEV, 16, HALF), BF16),
    ((1, 128), F32),
    ((DEV, 1, 128), F32),
    ((4 * CH, CH), BF16),
    ((CH, CH), BF16),
    ((CH, CH), BF16),
    ((CH, BINS), BF16),
    ((CH, 5 * CH), BF16),
    ((6 * CH, 1), F32),
    ((4 * CH, 1), F32),
    ((BINS, 1), F32),
)


def local(pair, labels, crop_length, *parameters):
    parameters = [p.reshape(1, -1) if p.ndim == 1 else p for p in parameters]
    parameters[10] = parameters[10].T
    grad, loss = pl.pallas_call(
        kernel,
        out_shape=(
            jax.ShapeDtypeStruct(pair.shape, BF16),
            jax.ShapeDtypeStruct((1, 128), F32),
        ),
        in_specs=[pl.BlockSpec(memory_space=pltpu.SMEM)]
        + [pl.BlockSpec(memory_space=pltpu.VMEM)] * (2 + len(parameters)),
        out_specs=[pl.BlockSpec(memory_space=pltpu.VMEM)] * 2,
        scratch_shapes=[pltpu.VMEM(shape, kind) for shape, kind in SCRATCH]
        + [pltpu.SemaphoreType.DMA((13,)), pltpu.SemaphoreType.DMA((13,))],
        compiler_params=pltpu.CompilerParams(
            collective_id=0, has_side_effects=True, vmem_limit_bytes=60 * 1024 * 1024
        ),
    )(crop_length, pair, labels, *parameters)
    return grad, loss[0, 0:1]


def solution(mesh):
    return jax.shard_map(
        local,
        mesh=mesh,
        in_specs=(P(("crop", "row"), None, None), P(("crop", "row"), None), P("crop")) + (P(),) * 12,
        out_specs=(P(("crop", "row"), None, None), P("crop")),
        check_vma=False,
    )
```

```python
import jax
import jax.numpy as jnp
from jax import lax
from jax.experimental import pallas as pl
from jax.experimental.pallas import tpu as pltpu
from jax.sharding import PartitionSpec as P

MESH = pl.DeviceIdType.MESH
F32 = jnp.float32
BF16 = jnp.bfloat16
DEV = 64
ROWS = 8
N = 512
HALF = 256
CH = 128
BINS = 64


def dot(a, b):
    return jnp.dot(a, b, preferred_element_type=F32)


def spaced_store(ref, at, x):
    for t in range(x.shape[1] // 128):
        ref.at[t][pl.ds(at, CH, 16), :] = x[:, t * 128 : (t + 1) * 128]


def tile_load(ref, runs, at, rows):
    rows = pl.ds(pl.multiple_of(at, 16), rows)
    return jnp.concatenate([ref[t, rows, :] for t in runs], axis=1)


def tile_store(ref, runs, at, x):
    rows = pl.ds(pl.multiple_of(at, 16), x.shape[0])
    for n, t in enumerate(runs):
        ref[t, rows, :] = x[:, n * 128 : (n + 1) * 128]


def each(count, body, unroll):
    def step(i, carry):
        body(i)
        return carry

    lax.fori_loop(0, count, step, 0, unroll=unroll)


def far_first():
    offsets = [
        (step % 4, (step // 4 + step) % 4, (step // 16 + step // 4 + step) % 4)
        for step in range(1, DEV)
    ]
    hops = lambda o: (0, 1, 2, 1)[o[0]] + (0, 1, 2, 1)[o[1]] + 2 * (o[2] // 2)
    offsets.sort(key=lambda o: -hops(o))
    codes = [o[0] * 16 + o[1] * 4 + o[2] for o in offsets]
    return [
        sum(code << (6 * n) for n, code in enumerate(codes[at : at + 5]))
        for at in range(0, len(codes), 5)
    ]


WORDS = far_first()


def partner(me, step):
    at = lax.div(step - 1, 5)
    word = jnp.int32(WORDS[0])
    for n in range(1, len(WORDS)):
        word = jnp.where(at == n, jnp.int32(WORDS[n]), word)
    code = (word >> (6 * lax.rem(step - 1, 5))) & 63
    depth = ((me >> 4) + (code >> 4)) & 3
    height = ((me >> 2) + (code >> 2)) & 3
    return depth * 16 + height * 4 + ((me & 3) ^ (code & 3))


def kernel(
    length_ref,
    pair_ref,
    labels_ref,
    in_gain_ref,
    in_bias_ref,
    proj_weight_ref,
    proj_bias_ref,
    gate_weight_ref,
    gate_bias_ref,
    mid_gain_ref,
    mid_bias_ref,
    out_weight_ref,
    out_shift_ref,
    dist_turned_ref,
    dist_bias_ref,
    grad_ref,
    loss_ref,
    values,
    in_hat,
    in_scale,
    normed,
    opened,
    amount,
    wide,
    send_planes,
    recv_planes,
    send_rest,
    recv_rest,
    left_ch,
    right_ch,
    send_product,
    recv_product,
    send_second,
    recv_second,
    mid,
    mid_hat,
    mid_scale,
    update,
    gate,
    logits,
    stack,
    send_logits,
    recv_logits,
    order,
    spread_order,
    row_order,
    cot,
    send_first,
    recv_first,
    send_grad,
    recv_grad,
    grad_mixed,
    grad_ch,
    send_back,
    recv_back,
    send_last,
    recv_last,
    part,
    parts,
    proj_t,
    gate_t,
    out_t,
    dist_weight,
    back_weight,
    columns,
    proj_column,
    dist_column,
    send_sem,
    recv_sem,
):
    me = lax.axis_index("row")
    length = length_ref[0]
    first_row = me * ROWS

    def greet(step, carry):
        pl.semaphore_signal(
            pltpu.get_barrier_semaphore(),
            inc=1,
            device_id={"row": partner(me, step)},
            device_id_type=MESH,
        )
        return carry

    lax.fori_loop(1, DEV, greet, 0)

    def send(slot, source, target, pack=None):
        def one(step, carry):
            peer = partner(me, step)
            if pack is not None:
                source.at[peer][...] = pack(peer)
            pltpu.make_async_remote_copy(
                src_ref=source.at[peer] if source.shape[0] == DEV else source,
                dst_ref=target.at[me],
                send_sem=send_sem.at[slot],
                recv_sem=recv_sem.at[slot],
                device_id={"row": peer},
                device_id_type=MESH,
            ).start()
            return carry

        lax.fori_loop(1, DEV, one, 0, unroll=3)
        if pack is not None:
            target.at[me][...] = pack(me)
        elif source.shape[0] == DEV:
            target.at[me][...] = source.at[me][...]
        else:
            target.at[me][...] = source[...]

    def arrived(slot, target):
        blocks = target.at[pl.ds(0, DEV - 1)]
        pltpu.make_async_copy(blocks, blocks, recv_sem.at[slot]).wait()

    def column(ref, out, at, size):
        out[pl.ds(at, size), :] = jnp.broadcast_to(ref[...], (8, size)).T[:, 0:1]

    column(in_gain_ref, columns, 0, CH)
    column(in_bias_ref, columns, CH, CH)
    column(proj_bias_ref, proj_column, 0, 4 * CH)
    proj_t[...] = proj_weight_ref[...].astype(F32).T.astype(BF16)

    lane = lax.broadcasted_iota(jnp.int32, (1, N), 1)

    def lanes(half):
        return slice(half * HALF, (half + 1) * HALF)

    def kept(i, half):
        row = jnp.full((1, HALF), first_row + i)
        return jnp.where((lane[:, lanes(half)] < length) & (row < length), 1.0, 0.0)

    def vec(k):
        return columns[pl.ds(k * CH, CH), :]

    def project(half):
        at = lanes(half)

        def body(i):
            x = pair_ref[i, at, :].astype(F32).T
            values[i, :, at] = x
            x = x - jnp.mean(x, axis=0, keepdims=True)
            scale = lax.rsqrt(jnp.mean(x * x, axis=0, keepdims=True) + 1e-05)
            x = x * scale
            in_hat[i, :, at] = x
            in_scale[i, :, at] = scale
            norm = (x * vec(0) + vec(1)).astype(BF16)
            normed[i, :, at] = norm
            keep = kept(i, half)
            for side in range(2):
                rows = pl.ds(2 * CH * side, 2 * CH)
                proj = dot(proj_t[rows, :], norm) + proj_column[rows, :]
                open_ = jax.nn.sigmoid(proj[0:CH])
                opened[side, i, :, at] = open_
                amount[side, i, :, at] = proj[CH:]
                spaced_store(
                    wide.at[pl.ds(2 * half, 2)], side * ROWS + i, open_ * proj[CH:] * keep
                )

        each(ROWS, body, ROWS)

    project(0)
    pl.semaphore_wait(pltpu.get_barrier_semaphore(), DEV - 1)
    send(
        0,
        send_planes,
        recv_planes,
        lambda d: tile_load(wide, (0, 1), d * 32, 32).astype(BF16).reshape(2, 16, HALF),
    )
    project(1)
    for odd in range(2):
        send(
            1 + odd,
            send_rest.at[odd],
            recv_rest.at[odd],
            lambda d: tile_load(wide, (2, 3), d * 32 + odd * 16, 16).astype(BF16),
        )

    column(gate_bias_ref, columns, 2 * CH, CH)
    column(mid_gain_ref, columns, 3 * CH, CH)
    column(mid_bias_ref, columns, 4 * CH, CH)
    column(out_shift_ref, columns, 5 * CH, CH)
    column(dist_bias_ref, dist_column, 0, BINS)
    gate_t[...] = gate_weight_ref[...].astype(F32).T.astype(BF16)
    out_t[...] = out_weight_ref[...].astype(F32).T.astype(BF16)
    dist_weight[...] = dist_turned_ref[...].astype(F32).T.astype(BF16)
    back_weight[:, 0 : 4 * CH] = proj_weight_ref[...]
    back_weight[:, 4 * CH : 5 * CH] = gate_weight_ref[...]
    row_at = lax.broadcasted_iota(jnp.int32, (N, N), 0)
    lane_at = lax.broadcasted_iota(jnp.int32, (N, N), 1)
    place = jnp.where(row_at < HALF, 2 * row_at, 2 * row_at - (N - 1))
    order[...] = jnp.where(place == lane_at, 1.0, 0.0).astype(BF16)
    place = (row_at & 7) * DEV + (row_at >> 3)
    spread_order[...] = jnp.where(place == lane_at, 1.0, 0.0).astype(BF16)
    place = ((row_at >> 2) & 1) * HALF + (row_at >> 3) * 4 + (row_at & 3)
    row_order[...] = jnp.where(place == lane_at, 1.0, 0.0).astype(BF16)

    def open_gate(i):
        gate[i] = jax.nn.sigmoid(dot(gate_t[...], normed[i]) + vec(2))

    each(ROWS, open_gate, 2)

    def unpack(odd, half, source):
        at = lanes(half)

        def body(b):
            block = source[pl.ds(b * 8, 8)].astype(F32).reshape(8, 2, 8, HALF)
            rows = pl.ds(pl.multiple_of(b * 64, 64), 64)
            left_ch[odd, rows, at] = block[:, 0].reshape(64, HALF).astype(BF16)
            right_ch[odd, rows, at] = block[:, 1].reshape(64, HALF).astype(BF16)

        each(8, body, 4)

    arrived(0, recv_planes)
    for odd in range(2):
        unpack(odd, 0, recv_planes.at[:, odd])

    def product(odd, half):
        x = lax.dot_general(
            left_ch[odd],
            right_ch[odd, lanes(half), :],
            (((1,), (1,)), ((), ())),
            preferred_element_type=F32,
        )
        return jnp.concatenate(
            [x[:, 0:128].reshape(DEV, 8, 128), x[:, 128:].reshape(DEV, 8, 128)], axis=1
        ).astype(BF16)

    arrived(1, recv_rest.at[0])
    unpack(0, 1, recv_rest.at[0])
    for half in range(2):
        send_product[:, half] = product(0, half)
    send(3, send_product, recv_product)
    arrived(2, recv_rest.at[1])
    unpack(1, 1, recv_rest.at[1])
    for half in range(2):
        send_second[half] = product(1, half)
        send(4 + half, send_second.at[half], recv_second.at[half])

    def mix(half):
        at = lanes(half)

        def body(i):
            x = jnp.concatenate(
                [mid.at[half][pl.ds(i, CH, 16), :], mid.at[half][pl.ds(8 + i, CH, 16), :]], axis=1
            )
            x = x - jnp.mean(x, axis=0, keepdims=True)
            scale = lax.rsqrt(jnp.mean(x * x, axis=0, keepdims=True) + 1e-05)
            x = x * scale
            mid_hat[i, :, at] = x
            mid_scale[i, :, at] = scale
            change = dot(out_t[...], (x * vec(3) + vec(4)).astype(BF16)) + vec(5)
            update[i, :, at] = change
            updated = (values[i, :, at] + gate[i, :, at] * change).astype(BF16)
            found = dot(dist_turned_ref[...], updated) + dist_column[...]
            logits[i, :, at] = found.astype(BF16).astype(F32)

        each(ROWS, body, 4)

    arrived(3, recv_product)
    for half in range(2):

        def spread(s):
            tile_store(mid, (half,), s * 32, recv_product[s, half].astype(F32))

        each(DEV, spread, 8)
    for half in range(2):
        arrived(4 + half, recv_second.at[half])

        def spread_second(s):
            tile_store(mid, (half,), s * 32 + 16, recv_second[half, s].astype(F32))

        each(DEV, spread_second, 8)
        mix(half)

    for p in range(4):
        pairs = jnp.concatenate([logits[2 * p], logits[2 * p + 1]], axis=0).astype(BF16)
        pairs = dot(pairs, spread_order[...]).T
        for i in range(ROWS):
            stack.at[i // 4][pl.ds(p * 4 + i % 4, DEV, 16), :] = pairs[i * DEV : (i + 1) * DEV]
    for four in range(2):
        send(
            6 + 7 * four,
            send_logits.at[four],
            recv_logits.at[four],
            lambda d: stack[four, pl.ds(pl.multiple_of(d * 16, 16), 16), :].astype(BF16),
        )

    part[...] = jnp.zeros_like(part)
    bin_at = lax.broadcasted_iota(jnp.int32, (BINS, HALF), 0)

    def backward(four, b):
        i = 4 * four + b
        turned = stack.at[four][pl.ds(b, HALF, 4), :].T.astype(BF16)
        turned = jnp.concatenate([turned[0:BINS], turned[BINS:]], axis=1)
        row = jnp.full((1, HALF), first_row + i)
        for half in range(2):
            at = lanes(half)
            sym = logits[i, :, at] + dot(turned, order[:, at])
            sym = sym - jnp.max(sym, axis=0, keepdims=True)
            logp = sym - jnp.log(jnp.sum(jnp.exp(sym), axis=0, keepdims=True))
            hot = jnp.where(labels_ref[pl.ds(i, 1), at] == bin_at, 1.0, 0.0)
            here = lane[:, at]
            live = (here < length) & (row < length) & (here != row)
            terms = -jnp.sum(hot * logp, axis=0, keepdims=True)
            terms = jnp.where(live & (here > row), terms, 0.0)
            part[...] += terms[:, 0:128] + terms[:, 128:]
            residue = jnp.where(live, jnp.exp(logp) - hot, 0.0).astype(BF16)
            back = dot(dist_weight[...], residue).astype(BF16)
            cot[i, :, at] = back
            back = (back.astype(F32) * gate[i, :, at]).astype(BF16)
            back = dot(out_weight_ref[...], back) * vec(3)
            hat = mid_hat[i, :, at]
            back = mid_scale[i, :, at] * (
                back
                - jnp.mean(back, axis=0, keepdims=True)
                - hat * jnp.mean(back * hat, axis=0, keepdims=True)
            )
            for t in range(2):
                rows = pl.ds(b * 4 + 2 * half + t, CH, 16)
                mid.at[four][rows, :] = back[:, t * 128 : (t + 1) * 128]

    for four in range(2):
        arrived(6 + 7 * four, recv_logits.at[four])
        stack[four] = recv_logits[four].astype(F32).reshape(DEV * 16, CH)
        each(4, lambda b: backward(four, b), 4)
        if four == 0:
            send(
                14,
                send_first,
                recv_first,
                lambda d: tile_load(mid, (0,), d * 32, 32).astype(BF16).reshape(2, 16, 128),
            )
    for odd in range(2):
        send(
            7 + odd,
            send_grad.at[odd],
            recv_grad.at[odd],
            lambda d: tile_load(mid, (1,), d * 32 + odd * 16, 16).astype(BF16),
        )
    send(9, part, parts)

    def planes_back(odd, half):
        at = lanes(half)
        x = dot(grad_ch[...], right_ch[odd, :, at]).reshape(DEV, 8, HALF)
        y = lax.dot_general(
            grad_ch[...], left_ch[odd, :, at], (((0,), (0,)), ((), ())), preferred_element_type=F32
        ).reshape(DEV, 8, HALF)
        return jnp.concatenate([x, y], axis=1).astype(BF16)

    for odd in range(2):
        for four in range(2):
            if four == 0:
                if odd == 0:
                    arrived(14, recv_first)
                stack[odd] = recv_first[:, odd].astype(F32).reshape(DEV * 16, 128)
            else:
                arrived(7 + odd, recv_grad.at[odd])
                stack[odd] = recv_grad[odd].astype(F32).reshape(DEV * 16, 128)
            for t in range(4):
                block = stack.at[odd][pl.ds(t, HALF, 4), :]
                grad_mixed[lanes(four), t * 128 : (t + 1) * 128] = block.astype(BF16)
        grad_ch[...] = dot(row_order[...], grad_mixed[...]).astype(BF16)
        for half in range(2):
            if odd == 0:
                send_back[:, :, lanes(half)] = planes_back(odd, half)
            else:
                send_last[half] = planes_back(odd, half)
                send(11 + half, send_last.at[half], recv_last.at[half])
        if odd == 0:
            send(10, send_back, recv_back)

    def finish(half):
        at = lanes(half)

        def body(i):
            keep = kept(i, half)
            pieces = []
            for side in range(2):
                rows = pl.ds(side * ROWS + i, CH, 16)
                grad = jnp.concatenate(
                    [wide.at[2 * half][rows, :], wide.at[2 * half + 1][rows, :]], axis=1
                )
                open_ = opened[side, i, :, at]
                grad = grad * keep * open_
                pieces.append((grad * amount[side, i, :, at] * (1.0 - open_)).astype(BF16))
                pieces.append(grad.astype(BF16))
            back = cot[i, :, at].astype(F32)
            open_ = gate[i, :, at]
            pieces.append((back * update[i, :, at] * open_ * (1.0 - open_)).astype(BF16))
            grad = dot(back_weight[...], jnp.concatenate(pieces, axis=0)) * vec(0)
            hat = in_hat[i, :, at]
            grad = in_scale[i, :, at] * (
                grad
                - jnp.mean(grad, axis=0, keepdims=True)
                - hat * jnp.mean(grad * hat, axis=0, keepdims=True)
            )
            grad_ref[i, at, :] = (grad + back).T.astype(BF16)

        each(ROWS, body, ROWS)

    arrived(10, recv_back)

    def spread_back(s):
        tile_store(wide, (0, 1, 2, 3), s * 32, recv_back[s].astype(F32))

    each(DEV, spread_back, 8)
    for half in range(2):
        arrived(11 + half, recv_last.at[half])

        def spread_last(s):
            tile_store(
                wide, (2 * half, 2 * half + 1), s * 32 + 16, recv_last[half, s].astype(F32)
            )

        each(DEV, spread_last, 8)
        finish(half)

    arrived(9, parts)
    total = jnp.sum(jnp.sum(parts[...], axis=0), axis=1, keepdims=True)
    present = jnp.full((1, 1), length).astype(F32)
    loss_ref[...] = jnp.broadcast_to(total / (present * (present - 1.0) / 2.0), (1, 128))

    for slot, blocks in (
        (0, send_planes),
        (1, send_rest.at[0]),
        (2, send_rest.at[1]),
        (3, send_product),
        (4, send_second.at[0]),
        (5, send_second.at[1]),
        (6, send_logits.at[0]),
        (13, send_logits.at[1]),
        (14, send_first),
        (7, send_grad.at[0]),
        (8, send_grad.at[1]),
        (9, parts),
        (10, send_back),
        (11, send_last.at[0]),
        (12, send_last.at[1]),
    ):
        blocks = blocks.at[pl.ds(0, DEV - 1)]
        pltpu.make_async_copy(blocks, blocks, send_sem.at[slot]).wait()


SCRATCH = (
    ((ROWS, CH, N), F32),
    ((ROWS, CH, N), F32),
    ((ROWS, 1, N), F32),
    ((ROWS, CH, N), BF16),
    ((2, ROWS, CH, N), F32),
    ((2, ROWS, CH, N), F32),
    ((4, CH * 16, 128), F32),
    ((DEV, 2, 16, HALF), BF16),
    ((DEV, 2, 16, HALF), BF16),
    ((2, DEV, 16, HALF), BF16),
    ((2, DEV, 16, HALF), BF16),
    ((2, N, N), BF16),
    ((2, N, N), BF16),
    ((DEV, 2, 16, 128), BF16),
    ((DEV, 2, 16, 128), BF16),
    ((2, DEV, 16, 128), BF16),
    ((2, DEV, 16, 128), BF16),
    ((2, CH * 16, 128), F32),
    ((ROWS, CH, N), F32),
    ((ROWS, 1, N), F32),
    ((ROWS, CH, N), F32),
    ((ROWS, CH, N), F32),
    ((ROWS, BINS, N), F32),
    ((2, DEV * 16, CH), F32),
    ((2, DEV, 16, CH), BF16),
    ((2, DEV, 16, CH), BF16),
    ((N, N), BF16),
    ((N, N), BF16),
    ((N, N), BF16),
    ((ROWS, CH, N), BF16),
    ((DEV, 2, 16, 128), BF16),
    ((DEV, 2, 16, 128), BF16),
    ((2, DEV, 16, 128), BF16),
    ((2, DEV, 16, 128), BF16),
    ((N, N), BF16),
    ((N, N), BF16),
    ((DEV, 16, N), BF16),
    ((DEV, 16, N), BF16),
    ((2, DEV, 16, HALF), BF16),
    ((2, DEV, 16, HALF), BF16),
    ((1, 128), F32),
    ((DEV, 1, 128), F32),
    ((4 * CH, CH), BF16),
    ((CH, CH), BF16),
    ((CH, CH), BF16),
    ((CH, BINS), BF16),
    ((CH, 5 * CH), BF16),
    ((6 * CH, 1), F32),
    ((4 * CH, 1), F32),
    ((BINS, 1), F32),
)


def local(pair, labels, crop_length, *parameters):
    parameters = [p.reshape(1, -1) if p.ndim == 1 else p for p in parameters]
    parameters[10] = parameters[10].T
    grad, loss = pl.pallas_call(
        kernel,
        out_shape=(
            jax.ShapeDtypeStruct(pair.shape, BF16),
            jax.ShapeDtypeStruct((1, 128), F32),
        ),
        in_specs=[pl.BlockSpec(memory_space=pltpu.SMEM)]
        + [pl.BlockSpec(memory_space=pltpu.VMEM)] * (2 + len(parameters)),
        out_specs=[pl.BlockSpec(memory_space=pltpu.VMEM)] * 2,
        scratch_shapes=[pltpu.VMEM(shape, kind) for shape, kind in SCRATCH]
        + [pltpu.SemaphoreType.DMA((15,)), pltpu.SemaphoreType.DMA((15,))],
        compiler_params=pltpu.CompilerParams(
            collective_id=0, has_side_effects=True, vmem_limit_bytes=60 * 1024 * 1024
        ),
    )(crop_length, pair, labels, *parameters)
    return grad, loss[0, 0:1]


def solution(mesh):
    return jax.shard_map(
        local,
        mesh=mesh,
        in_specs=(P(("crop", "row"), None, None), P(("crop", "row"), None), P("crop")) + (P(),) * 12,
        out_specs=(P(("crop", "row"), None, None), P("crop")),
        check_vma=False,
    )
```

```python
import jax
import jax.numpy as jnp
from jax import lax
from jax.experimental import pallas as pl
from jax.experimental.pallas import tpu as pltpu
from jax.sharding import PartitionSpec as P

MESH = pl.DeviceIdType.MESH
F32 = jnp.float32
BF16 = jnp.bfloat16
DEV = 64
ROWS = 8
N = 512
HALF = 256
CH = 128
BINS = 64


def dot(a, b):
    return jnp.dot(a, b, preferred_element_type=F32)


def spaced_store(ref, at, x):
    for t in range(x.shape[1] // 128):
        ref.at[t][pl.ds(at, CH, 16), :] = x[:, t * 128 : (t + 1) * 128]


def tile_load(ref, runs, at, rows):
    rows = pl.ds(pl.multiple_of(at, 16), rows)
    return jnp.concatenate([ref[t, rows, :] for t in runs], axis=1)


def tile_store(ref, runs, at, x):
    rows = pl.ds(pl.multiple_of(at, 16), x.shape[0])
    for n, t in enumerate(runs):
        ref[t, rows, :] = x[:, n * 128 : (n + 1) * 128]


def each(count, body, unroll):
    def step(i, carry):
        body(i)
        return carry

    lax.fori_loop(0, count, step, 0, unroll=unroll)


def far_first():
    offsets = [
        (step % 4, (step // 4 + step) % 4, (step // 16 + step // 4 + step) % 4)
        for step in range(1, DEV)
    ]
    hops = lambda o: (0, 1, 2, 1)[o[0]] + (0, 1, 2, 1)[o[1]] + 2 * (o[2] // 2)
    offsets.sort(key=lambda o: -hops(o))
    codes = [o[0] * 16 + o[1] * 4 + o[2] for o in offsets]
    return [
        sum(code << (6 * n) for n, code in enumerate(codes[at : at + 3]))
        for at in range(0, len(codes), 3)
    ]


WORDS = far_first()


def partners(me, at):
    word = jnp.int32(WORDS[0])
    for n in range(1, len(WORDS)):
        word = jnp.where(at == n, jnp.int32(WORDS[n]), word)
    found = []
    for n in range(3):
        depth = ((me >> 4) + (word >> (6 * n + 4))) & 3
        height = ((me >> 2) + (word >> (6 * n + 2))) & 3
        found.append(depth * 16 + height * 4 + ((me ^ (word >> (6 * n))) & 3))
    return found


def kernel(
    length_ref,
    pair_ref,
    labels_ref,
    in_gain_ref,
    in_bias_ref,
    proj_weight_ref,
    proj_bias_ref,
    gate_weight_ref,
    gate_bias_ref,
    mid_gain_ref,
    mid_bias_ref,
    out_weight_ref,
    out_shift_ref,
    dist_turned_ref,
    dist_bias_ref,
    grad_ref,
    loss_ref,
    values,
    in_hat,
    in_scale,
    normed,
    opened,
    amount,
    wide,
    send_planes,
    recv_planes,
    send_rest,
    recv_rest,
    left_ch,
    right_ch,
    send_product,
    recv_product,
    send_second,
    recv_second,
    mid,
    mid_hat,
    mid_scale,
    update,
    gate,
    logits,
    stack,
    send_logits,
    recv_logits,
    order,
    spread_order,
    row_order,
    cot,
    send_first,
    recv_first,
    send_grad,
    recv_grad,
    grad_mixed,
    grad_ch,
    send_back,
    recv_back,
    send_last,
    recv_last,
    part,
    parts,
    proj_t,
    gate_t,
    out_t,
    dist_weight,
    back_weight,
    columns,
    proj_column,
    dist_column,
    send_sem,
    recv_sem,
):
    me = lax.axis_index("row")
    length = length_ref[0]
    first_row = me * ROWS

    def greet(step, carry):
        pl.semaphore_signal(
            pltpu.get_barrier_semaphore(),
            inc=1,
            device_id={"row": (me + step) & (DEV - 1)},
            device_id_type=MESH,
        )
        return carry

    lax.fori_loop(1, DEV, greet, 0)

    def send(slot, source, target, pack=None):
        def three(at):
            for peer in partners(me, at):
                if pack is not None:
                    source.at[peer][...] = pack(peer)
                pltpu.make_async_remote_copy(
                    src_ref=source.at[peer] if source.shape[0] == DEV else source,
                    dst_ref=target.at[me],
                    send_sem=send_sem.at[slot],
                    recv_sem=recv_sem.at[slot],
                    device_id={"row": peer},
                    device_id_type=MESH,
                ).start()

        each(len(WORDS), three, 1)
        if pack is not None:
            target.at[me][...] = pack(me)
        elif source.shape[0] == DEV:
            target.at[me][...] = source.at[me][...]
        else:
            target.at[me][...] = source[...]

    def arrived(slot, target):
        blocks = target.at[pl.ds(0, DEV - 1)]
        pltpu.make_async_copy(blocks, blocks, recv_sem.at[slot]).wait()

    def column(ref, out, at, size):
        out[pl.ds(at, size), :] = jnp.broadcast_to(ref[...], (8, size)).T[:, 0:1]

    column(in_gain_ref, columns, 0, CH)
    column(in_bias_ref, columns, CH, CH)
    column(proj_bias_ref, proj_column, 0, 4 * CH)
    proj_t[...] = proj_weight_ref[...].astype(F32).T.astype(BF16)

    lane = lax.broadcasted_iota(jnp.int32, (1, N), 1)

    def lanes(half):
        return slice(half * HALF, (half + 1) * HALF)

    def kept(i, half):
        row = jnp.full((1, HALF), first_row + i)
        return jnp.where((lane[:, lanes(half)] < length) & (row < length), 1.0, 0.0)

    def vec(k):
        return columns[pl.ds(k * CH, CH), :]

    def project(half):
        at = lanes(half)

        def body(i):
            x = pair_ref[i, at, :].astype(F32).T
            values[i, :, at] = x
            x = x - jnp.mean(x, axis=0, keepdims=True)
            scale = lax.rsqrt(jnp.mean(x * x, axis=0, keepdims=True) + 1e-05)
            x = x * scale
            in_hat[i, :, at] = x
            in_scale[i, :, at] = scale
            norm = (x * vec(0) + vec(1)).astype(BF16)
            normed[i, :, at] = norm
            keep = kept(i, half)
            for side in range(2):
                rows = pl.ds(2 * CH * side, 2 * CH)
                proj = dot(proj_t[rows, :], norm) + proj_column[rows, :]
                open_ = jax.nn.sigmoid(proj[0:CH])
                opened[side, i, :, at] = open_
                amount[side, i, :, at] = proj[CH:]
                spaced_store(
                    wide.at[pl.ds(2 * half, 2)], side * ROWS + i, open_ * proj[CH:] * keep
                )

        each(ROWS, body, ROWS)

    project(0)
    pl.semaphore_wait(pltpu.get_barrier_semaphore(), DEV - 1)
    send(
        0,
        send_planes,
        recv_planes,
        lambda d: tile_load(wide, (0, 1), d * 32, 32).astype(BF16).reshape(2, 16, HALF),
    )
    project(1)
    for odd in range(2):
        send(
            1 + odd,
            send_rest.at[odd],
            recv_rest.at[odd],
            lambda d: tile_load(wide, (2, 3), d * 32 + odd * 16, 16).astype(BF16),
        )

    column(gate_bias_ref, columns, 2 * CH, CH)
    column(mid_gain_ref, columns, 3 * CH, CH)
    column(mid_bias_ref, columns, 4 * CH, CH)
    column(out_shift_ref, columns, 5 * CH, CH)
    column(dist_bias_ref, dist_column, 0, BINS)
    gate_t[...] = gate_weight_ref[...].astype(F32).T.astype(BF16)
    out_t[...] = out_weight_ref[...].astype(F32).T.astype(BF16)
    dist_weight[...] = dist_turned_ref[...].astype(F32).T.astype(BF16)
    back_weight[:, 0 : 4 * CH] = proj_weight_ref[...]
    back_weight[:, 4 * CH : 5 * CH] = gate_weight_ref[...]
    row_at = lax.broadcasted_iota(jnp.int32, (N, N), 0)
    lane_at = lax.broadcasted_iota(jnp.int32, (N, N), 1)
    place = jnp.where(row_at < HALF, 2 * row_at, 2 * row_at - (N - 1))
    order[...] = jnp.where(place == lane_at, 1.0, 0.0).astype(BF16)
    place = (row_at & 7) * DEV + (row_at >> 3)
    spread_order[...] = jnp.where(place == lane_at, 1.0, 0.0).astype(BF16)
    place = ((row_at >> 2) & 1) * HALF + (row_at >> 3) * 4 + (row_at & 3)
    row_order[...] = jnp.where(place == lane_at, 1.0, 0.0).astype(BF16)

    def open_gate(i):
        gate[i] = jax.nn.sigmoid(dot(gate_t[...], normed[i]) + vec(2))

    each(ROWS, open_gate, 2)

    def unpack(odd, half, source):
        at = lanes(half)

        def body(b):
            block = source[pl.ds(b * 8, 8)].astype(F32).reshape(8, 2, 8, HALF)
            rows = pl.ds(pl.multiple_of(b * 64, 64), 64)
            left_ch[odd, rows, at] = block[:, 0].reshape(64, HALF).astype(BF16)
            right_ch[odd, rows, at] = block[:, 1].reshape(64, HALF).astype(BF16)

        each(8, body, 4)

    arrived(0, recv_planes)
    for odd in range(2):
        unpack(odd, 0, recv_planes.at[:, odd])

    def product(odd, half):
        x = lax.dot_general(
            left_ch[odd],
            right_ch[odd, lanes(half), :],
            (((1,), (1,)), ((), ())),
            preferred_element_type=F32,
        )
        return jnp.concatenate(
            [x[:, 0:128].reshape(DEV, 8, 128), x[:, 128:].reshape(DEV, 8, 128)], axis=1
        ).astype(BF16)

    arrived(1, recv_rest.at[0])
    unpack(0, 1, recv_rest.at[0])
    for half in range(2):
        send_product[:, half] = product(0, half)
    send(3, send_product, recv_product)
    arrived(2, recv_rest.at[1])
    unpack(1, 1, recv_rest.at[1])
    for half in range(2):
        send_second[half] = product(1, half)
        send(4 + half, send_second.at[half], recv_second.at[half])

    def mix(half):
        at = lanes(half)

        def body(i):
            x = jnp.concatenate(
                [mid.at[half][pl.ds(i, CH, 16), :], mid.at[half][pl.ds(8 + i, CH, 16), :]], axis=1
            )
            x = x - jnp.mean(x, axis=0, keepdims=True)
            scale = lax.rsqrt(jnp.mean(x * x, axis=0, keepdims=True) + 1e-05)
            x = x * scale
            mid_hat[i, :, at] = x
            mid_scale[i, :, at] = scale
            change = dot(out_t[...], (x * vec(3) + vec(4)).astype(BF16)) + vec(5)
            update[i, :, at] = change
            updated = (values[i, :, at] + gate[i, :, at] * change).astype(BF16)
            found = dot(dist_turned_ref[...], updated) + dist_column[...]
            logits[i, :, at] = found.astype(BF16).astype(F32)

        each(ROWS, body, 4)

    arrived(3, recv_product)
    for half in range(2):

        def spread(s):
            tile_store(mid, (half,), s * 32, recv_product[s, half].astype(F32))

        each(DEV, spread, 8)
    for half in range(2):
        arrived(4 + half, recv_second.at[half])

        def spread_second(s):
            tile_store(mid, (half,), s * 32 + 16, recv_second[half, s].astype(F32))

        each(DEV, spread_second, 8)
        mix(half)

    for p in range(4):
        pairs = jnp.concatenate([logits[2 * p], logits[2 * p + 1]], axis=0).astype(BF16)
        pairs = dot(pairs, spread_order[...]).T
        for i in range(ROWS):
            stack.at[i // 4][pl.ds(p * 4 + i % 4, DEV, 16), :] = pairs[i * DEV : (i + 1) * DEV]
    for four in range(2):
        send(
            6 + 7 * four,
            send_logits.at[four],
            recv_logits.at[four],
            lambda d: stack[four, pl.ds(pl.multiple_of(d * 16, 16), 16), :].astype(BF16),
        )

    part[...] = jnp.zeros_like(part)
    bin_at = lax.broadcasted_iota(jnp.int32, (BINS, HALF), 0)

    def backward(four, b):
        i = 4 * four + b
        turned = stack.at[four][pl.ds(b, HALF, 4), :].T.astype(BF16)
        turned = jnp.concatenate([turned[0:BINS], turned[BINS:]], axis=1)
        row = jnp.full((1, HALF), first_row + i)
        for half in range(2):
            at = lanes(half)
            sym = logits[i, :, at] + dot(turned, order[:, at])
            sym = sym - jnp.max(sym, axis=0, keepdims=True)
            logp = sym - jnp.log(jnp.sum(jnp.exp(sym), axis=0, keepdims=True))
            hot = jnp.where(labels_ref[pl.ds(i, 1), at] == bin_at, 1.0, 0.0)
            here = lane[:, at]
            live = (here < length) & (row < length) & (here != row)
            terms = -jnp.sum(hot * logp, axis=0, keepdims=True)
            terms = jnp.where(live & (here > row), terms, 0.0)
            part[...] += terms[:, 0:128] + terms[:, 128:]
            residue = jnp.where(live, jnp.exp(logp) - hot, 0.0).astype(BF16)
            back = dot(dist_weight[...], residue).astype(BF16)
            cot[i, :, at] = back
            back = (back.astype(F32) * gate[i, :, at]).astype(BF16)
            back = dot(out_weight_ref[...], back) * vec(3)
            hat = mid_hat[i, :, at]
            back = mid_scale[i, :, at] * (
                back
                - jnp.mean(back, axis=0, keepdims=True)
                - hat * jnp.mean(back * hat, axis=0, keepdims=True)
            )
            for t in range(2):
                rows = pl.ds(b * 4 + 2 * half + t, CH, 16)
                mid.at[four][rows, :] = back[:, t * 128 : (t + 1) * 128]

    for four in range(2):
        arrived(6 + 7 * four, recv_logits.at[four])
        stack[four] = recv_logits[four].astype(F32).reshape(DEV * 16, CH)
        each(4, lambda b: backward(four, b), 4)
        if four == 0:
            send(
                14,
                send_first,
                recv_first,
                lambda d: tile_load(mid, (0,), d * 32, 32).astype(BF16).reshape(2, 16, 128),
            )
    for odd in range(2):
        send(
            7 + odd,
            send_grad.at[odd],
            recv_grad.at[odd],
            lambda d: tile_load(mid, (1,), d * 32 + odd * 16, 16).astype(BF16),
        )

    def planes_back(odd, half):
        at = lanes(half)
        x = dot(grad_ch[...], right_ch[odd, :, at]).reshape(DEV, 8, HALF)
        y = lax.dot_general(
            grad_ch[...], left_ch[odd, :, at], (((0,), (0,)), ((), ())), preferred_element_type=F32
        ).reshape(DEV, 8, HALF)
        return jnp.concatenate([x, y], axis=1).astype(BF16)

    for odd in range(2):
        for four in range(2):
            if four == 0:
                if odd == 0:
                    arrived(14, recv_first)
                stack[odd] = recv_first[:, odd].astype(F32).reshape(DEV * 16, 128)
            else:
                arrived(7 + odd, recv_grad.at[odd])
                stack[odd] = recv_grad[odd].astype(F32).reshape(DEV * 16, 128)
            for t in range(4):
                block = stack.at[odd][pl.ds(t, HALF, 4), :]
                grad_mixed[lanes(four), t * 128 : (t + 1) * 128] = block.astype(BF16)
        grad_ch[...] = dot(row_order[...], grad_mixed[...]).astype(BF16)
        for half in range(2):
            if odd == 0:
                send_back[:, :, lanes(half)] = planes_back(odd, half)
            else:
                send_last[half] = planes_back(odd, half)
                send(11 + half, send_last.at[half], recv_last.at[half])
        if odd == 0:
            send(10, send_back, recv_back)
            send(9, part, parts)

    def finish(half):
        at = lanes(half)

        def body(i):
            keep = kept(i, half)
            pieces = []
            for side in range(2):
                rows = pl.ds(side * ROWS + i, CH, 16)
                grad = jnp.concatenate(
                    [wide.at[2 * half][rows, :], wide.at[2 * half + 1][rows, :]], axis=1
                )
                open_ = opened[side, i, :, at]
                grad = grad * keep * open_
                pieces.append((grad * amount[side, i, :, at] * (1.0 - open_)).astype(BF16))
                pieces.append(grad.astype(BF16))
            back = cot[i, :, at].astype(F32)
            open_ = gate[i, :, at]
            pieces.append((back * update[i, :, at] * open_ * (1.0 - open_)).astype(BF16))
            grad = dot(back_weight[...], jnp.concatenate(pieces, axis=0)) * vec(0)
            hat = in_hat[i, :, at]
            grad = in_scale[i, :, at] * (
                grad
                - jnp.mean(grad, axis=0, keepdims=True)
                - hat * jnp.mean(grad * hat, axis=0, keepdims=True)
            )
            grad_ref[i, at, :] = (grad + back).T.astype(BF16)

        each(ROWS, body, ROWS)

    arrived(10, recv_back)

    def spread_back(s):
        tile_store(wide, (0, 1, 2, 3), s * 32, recv_back[s].astype(F32))

    each(DEV, spread_back, 8)
    for half in range(2):
        arrived(11 + half, recv_last.at[half])

        def spread_last(s):
            tile_store(
                wide, (2 * half, 2 * half + 1), s * 32 + 16, recv_last[half, s].astype(F32)
            )

        each(DEV, spread_last, 8)
        finish(half)

    arrived(9, parts)
    total = jnp.sum(jnp.sum(parts[...], axis=0), axis=1, keepdims=True)
    present = jnp.full((1, 1), length).astype(F32)
    loss_ref[...] = jnp.broadcast_to(total / (present * (present - 1.0) / 2.0), (1, 128))

    for slot, blocks in (
        (0, send_planes),
        (1, send_rest.at[0]),
        (2, send_rest.at[1]),
        (3, send_product),
        (4, send_second.at[0]),
        (5, send_second.at[1]),
        (6, send_logits.at[0]),
        (13, send_logits.at[1]),
        (14, send_first),
        (7, send_grad.at[0]),
        (8, send_grad.at[1]),
        (9, parts),
        (10, send_back),
        (11, send_last.at[0]),
        (12, send_last.at[1]),
    ):
        blocks = blocks.at[pl.ds(0, DEV - 1)]
        pltpu.make_async_copy(blocks, blocks, send_sem.at[slot]).wait()


SCRATCH = (
    ((ROWS, CH, N), F32),
    ((ROWS, CH, N), F32),
    ((ROWS, 1, N), F32),
    ((ROWS, CH, N), BF16),
    ((2, ROWS, CH, N), F32),
    ((2, ROWS, CH, N), F32),
    ((4, CH * 16, 128), F32),
    ((DEV, 2, 16, HALF), BF16),
    ((DEV, 2, 16, HALF), BF16),
    ((2, DEV, 16, HALF), BF16),
    ((2, DEV, 16, HALF), BF16),
    ((2, N, N), BF16),
    ((2, N, N), BF16),
    ((DEV, 2, 16, 128), BF16),
    ((DEV, 2, 16, 128), BF16),
    ((2, DEV, 16, 128), BF16),
    ((2, DEV, 16, 128), BF16),
    ((2, CH * 16, 128), F32),
    ((ROWS, CH, N), F32),
    ((ROWS, 1, N), F32),
    ((ROWS, CH, N), F32),
    ((ROWS, CH, N), F32),
    ((ROWS, BINS, N), F32),
    ((2, DEV * 16, CH), F32),
    ((2, DEV, 16, CH), BF16),
    ((2, DEV, 16, CH), BF16),
    ((N, N), BF16),
    ((N, N), BF16),
    ((N, N), BF16),
    ((ROWS, CH, N), BF16),
    ((DEV, 2, 16, 128), BF16),
    ((DEV, 2, 16, 128), BF16),
    ((2, DEV, 16, 128), BF16),
    ((2, DEV, 16, 128), BF16),
    ((N, N), BF16),
    ((N, N), BF16),
    ((DEV, 16, N), BF16),
    ((DEV, 16, N), BF16),
    ((2, DEV, 16, HALF), BF16),
    ((2, DEV, 16, HALF), BF16),
    ((1, 128), F32),
    ((DEV, 1, 128), F32),
    ((4 * CH, CH), BF16),
    ((CH, CH), BF16),
    ((CH, CH), BF16),
    ((CH, BINS), BF16),
    ((CH, 5 * CH), BF16),
    ((6 * CH, 1), F32),
    ((4 * CH, 1), F32),
    ((BINS, 1), F32),
)


def local(pair, labels, crop_length, *parameters):
    parameters = [p.reshape(1, -1) if p.ndim == 1 else p for p in parameters]
    parameters[10] = parameters[10].T
    grad, loss = pl.pallas_call(
        kernel,
        out_shape=(
            jax.ShapeDtypeStruct(pair.shape, BF16),
            jax.ShapeDtypeStruct((1, 128), F32),
        ),
        in_specs=[pl.BlockSpec(memory_space=pltpu.SMEM)]
        + [pl.BlockSpec(memory_space=pltpu.VMEM)] * (2 + len(parameters)),
        out_specs=[pl.BlockSpec(memory_space=pltpu.VMEM)] * 2,
        scratch_shapes=[pltpu.VMEM(shape, kind) for shape, kind in SCRATCH]
        + [pltpu.SemaphoreType.DMA((15,)), pltpu.SemaphoreType.DMA((15,))],
        compiler_params=pltpu.CompilerParams(
            collective_id=0, has_side_effects=True, vmem_limit_bytes=60 * 1024 * 1024
        ),
    )(crop_length, pair, labels, *parameters)
    return grad, loss[0, 0:1]


def solution(mesh):
    return jax.shard_map(
        local,
        mesh=mesh,
        in_specs=(P(("crop", "row"), None, None), P(("crop", "row"), None), P("crop")) + (P(),) * 12,
        out_specs=(P(("crop", "row"), None, None), P("crop")),
        check_vma=False,
    )
```
